32 devices in a mesh: grp: 2 (over y), row: 4 (over z), sub: 4 (over x, core).
Axes of the slice: x: 2, y: 2, z: 4, core: 2. Of those that a mesh axis runs over, the one named last changes fastest.
Arguments:
- observed: float32 [512, 128], P(('grp', 'row')), parts along dimension 0, may hold values from -18 to 18
- sens_tiles: bfloat16 [8, 4, 128, 64, 128], P(('grp', 'row'), 'sub'), parts along dimension 0, may hold values from -0.25 to 0.25
- tile_row: int32 [8, 4, 128], P(('grp', 'row'), 'sub'), parts along dimension 0, may hold values from 0 to 63
- tile_owner: int32 [8, 4, 128], P(('grp', 'row'), 'sub'), parts along dimension 0, may hold values from 0 to 3, as said below
- tile_block: int32 [8, 4, 128], P(('grp', 'row'), 'sub'), parts along dimension 0, may hold values from 0 to 1023
- coeffs: float32 [512, 64, 64], P(('grp', 'row'), 'sub'), parts along dimension 0, may hold values from -6 to 6
- split_var: float32 [128, 64, 256], P(('grp', 'row'), 'sub'), parts along dimension 0, may hold values from -3.15 to 3.15, as said below
- scaled_dual: float32 [128, 64, 256], P(('grp', 'row'), 'sub'), parts along dimension 0, may hold values from -16.2 to 16.2
- lower_bound: float32 [128, 64, 256], P(('grp', 'row'), 'sub'), parts along dimension 0, may hold values from -10.8 to -0.4
- upper_bound: float32 [128, 64, 256], P(('grp', 'row'), 'sub'), parts along dimension 0, may hold values from 0.4 to 10.8
Outputs:
- model_next: float32 [128, 64, 256], P(('grp', 'row'), 'sub'), parts along dimension 0
- split_next: float32 [128, 64, 256], P(('grp', 'row'), 'sub'), parts along dimension 0
- dual_next: float32 [128, 64, 256], P(('grp', 'row'), 'sub'), parts along dimension 0
- residual_norms: float32 [6], P('grp'), parts along dimension 0
The draws below stay inside these ranges and needn't reach their ends.
There are 2 independent parts, one for each index of `grp`. The reference program is written for one: setup_inputs(seed, part) draws one part's arguments, and reference() takes and returns one part's arrays. A program takes and returns all parts, laid end to end along the dimension named above; each array names one. Nothing has to cross between parts.
Inputs may be any that keep to these rules, and one draw needn't show every extreme that they name: `tile_owner`: within one device's list (fixed r and s), at most 96 tiles name the same owner row; in each sub column one owner row is named exactly 96 times in every device's list. lower_bound <= split_var <= upper_bound in every cell.
All inputs are finite; a program needn't handle non-finite values.
Results may differ from the reference program's by a relative error of at most 0.0028.
Values may be sent and summed in bfloat16 or wider, within the bound.
A program may use at most 64 MiB of HBM per device.

```python
import math
import jax
import jax.numpy as jnp
import numpy as np
from jax import lax

TR = 128
TC = 64
LEVELS = 3
CY = 16
NZ = 256
TILES_DEV = 128
ROWB = 64
NX = 64
NY = 64
CZC = 64
BLK_DEV = 1024
CAP = 96
N_ROW = 4
N_SUB = 4


def rising(length_all, growth):
    return growth ** (jnp.arange(length_all, dtype=jnp.float32) / (length_all - 1))


def cell_scale(growth):
    return rising(NX, growth)[:, None, None]


def draw_observed(key, part):
    key = jax.random.fold_in(key, 5)
    col_key, val_key = jax.random.split(key, 2)
    total_rows = N_ROW * ROWB
    column_scale = jnp.exp(jax.random.uniform(col_key, (1, TR), jnp.float32, jnp.log(0.5), jnp.log(2.0)))
    growth = 3.0
    base_draw = 0.5 * jax.random.truncated_normal(val_key, -4.0, 4.0, (total_rows, TR), jnp.float32)
    return rising(total_rows, growth)[:, None] * column_scale * base_draw


def draw_lower_bound(key, part):
    key = jax.random.fold_in(key, 7)
    growth = 3.0
    base_draw = jax.random.uniform(key, (NX, NY, NZ), jnp.float32, 0.4, 1.2)
    return -cell_scale(growth) * base_draw


def draw_upper_bound(key, part):
    key = jax.random.fold_in(key, 9)
    growth = 3.0
    base_draw = jax.random.uniform(key, (NX, NY, NZ), jnp.float32, 0.4, 1.2)
    return cell_scale(growth) * base_draw


def draw_split_var(key, part):
    key = jax.random.fold_in(key, 11)
    growth = 3.0
    base_draw = jax.random.uniform(key, (NX, NY, NZ), jnp.float32, -0.35, 0.35)
    return cell_scale(growth) * base_draw


def draw_scaled_dual(key, part):
    key = jax.random.fold_in(key, 13)
    depth_key, val_key = jax.random.split(key, 2)
    depth_scale = jnp.exp(jax.random.uniform(depth_key, (1, 1, NZ), jnp.float32, jnp.log(0.3), jnp.log(3.0)))
    growth = 3.0
    base_draw = jax.random.truncated_normal(val_key, -3.0, 3.0, (NX, NY, NZ), jnp.float32)
    return 0.4 * cell_scale(growth) * depth_scale * base_draw


def draw_tile_owner(key, part):
    key = jax.random.fold_in(key, 31)
    hot_key, rank_key, noise_key, order_key = jax.random.split(key, 4)
    hot_rows = jax.random.randint(hot_key, (N_SUB,), 0, N_ROW)
    ranks = jax.vmap(lambda sub_key: jax.random.permutation(sub_key, N_ROW))(jax.random.split(rank_key, N_SUB))
    noise = jax.random.randint(noise_key, (N_ROW, N_SUB, N_ROW, CAP), 0, 2 * N_ROW)
    owner_grid = jnp.arange(N_ROW, dtype=jnp.int32)[None, None, :, None]
    is_hot = owner_grid == hot_rows[None, :, None, None]
    score = jnp.where(is_hot, 4 * N_ROW, ranks[None, :, :, None] + noise)
    slot_grid = jnp.arange(N_ROW * CAP, dtype=jnp.int32).reshape(N_ROW, CAP)
    score = score * (N_ROW * CAP) + slot_grid[None, None]
    flat_score = score.reshape(N_ROW, N_SUB, N_ROW * CAP)
    chosen = jax.lax.top_k(flat_score, TILES_DEV)[1] // CAP
    order_score = jax.random.randint(order_key, (N_ROW, N_SUB, TILES_DEV), 0, 1 << 20) * TILES_DEV
    order_score = order_score + jnp.arange(TILES_DEV, dtype=jnp.int32)[None, None, :]
    order = jnp.argsort(order_score, axis=-1, stable=True)
    return jnp.take_along_axis(chosen, order, axis=-1).astype(jnp.int32)


def set_ends(drawn, rng, smallest, top_value):
    longest = drawn.shape.index(max(drawn.shape))
    spots = []
    for shift in (0, 1):
        where = [jax.random.randint(jax.random.fold_in(rng, axis), (), 0, length) for axis, length in enumerate(drawn.shape)]
        where[longest] = (where[longest] + shift) % drawn.shape[longest]
        spots.append(tuple(where))
    return drawn.at[spots[0]].set(smallest).at[spots[1]].set(top_value)


def steps_of(stream_key, extent, cuts, smallest, high):
    def one(position, shards_of):
        steps = jax.random.uniform(jax.random.fold_in(jax.random.fold_in(stream_key, 6), position), (shards_of,), jnp.float32, smallest / len(cuts), high / len(cuts))
        return jnp.repeat(jnp.exp(steps), extent[position] // shards_of).reshape((-1,) + (1,) * (len(extent) - position - 1))

    level = one(*cuts[0])
    for cut in cuts[1:]:
        level = level * one(*cut)
    return level


def rank_table(number_of, lean):
    loads = [(1 << 20) // math.isqrt(rank ** lean) + 1 for rank in range(1, number_of + 1)]
    deviation = 1 + sum(loads) // (1 << 30)
    return np.cumsum(np.array([max(1, weight // deviation) for weight in loads]))


def ranked_ids(rng, dims, amount, skew):
    grid = rank_table(amount, skew)
    lot = jax.random.randint(jax.random.fold_in(rng, 1), dims, 0, int(grid[amount - 1]))
    grade = jnp.searchsorted(jnp.asarray(grid, jnp.int32), lot, side="right")
    return jax.random.permutation(jax.random.fold_in(rng, 2), amount)[grade].astype(jnp.int32)


def gaussian(key, dims, spread, limit, cuts=(), held_as=jnp.bfloat16):
    factor_of = steps_of(key, dims, cuts, -0.22, 0.18) if cuts else 1.0
    result = jax.random.normal(key, dims, jnp.float32) * spread * factor_of
    return jnp.minimum(jnp.maximum(result, -limit), limit).astype(held_as)


def setup_inputs(seed: int = 0, part: int = 0) -> dict:
    seeds = jax.random.split(jax.random.key(seed), 11)
    part_keys = jax.random.split(jax.random.fold_in(seeds[10], part), 11)
    observed = draw_observed(jax.random.fold_in(jax.random.fold_in(seeds[10], part), 71), part)
    sens_tiles = gaussian(part_keys[1], (N_ROW, N_SUB, TILES_DEV, TC, TR), (TC * N_SUB * TILES_DEV // ROWB) ** -0.5, 0.25, ((0, 4), (1, 4)))
    tile_row = set_ends(jax.random.randint(part_keys[2], (N_ROW, N_SUB, TILES_DEV), 0, ROWB), jax.random.fold_in(part_keys[2], 1), 0, ROWB - 1).astype(jnp.int32)
    tile_owner = draw_tile_owner(jax.random.fold_in(jax.random.fold_in(seeds[10], part), 71), part)
    tile_block = set_ends(ranked_ids(part_keys[4], (N_ROW, N_SUB, TILES_DEV), BLK_DEV, 2), jax.random.fold_in(part_keys[4], 3), 0, BLK_DEV - 1).astype(jnp.int32)
    coeffs = gaussian(part_keys[5], (NZ, NY, NX), 1.0, 6.0, ((0, 4), (1, 4)), jnp.float32)
    split_var = draw_split_var(jax.random.fold_in(jax.random.fold_in(seeds[10], part), 71), part)
    scaled_dual = draw_scaled_dual(jax.random.fold_in(jax.random.fold_in(seeds[10], part), 71), part)
    lower_bound = draw_lower_bound(jax.random.fold_in(jax.random.fold_in(seeds[10], part), 71), part)
    upper_bound = draw_upper_bound(jax.random.fold_in(jax.random.fold_in(seeds[10], part), 71), part)
    return {"observed": observed, "sens_tiles": sens_tiles, "tile_row": tile_row, "tile_owner": tile_owner, "tile_block": tile_block, "coeffs": coeffs, "split_var": split_var, "scaled_dual": scaled_dual, "lower_bound": lower_bound, "upper_bound": upper_bound}


half_root = 0.7071067811865476
step_size = 0.1
smooth_weight = 0.5
data_weight = 20.0
penalty = 1.0

def synthesis(coef_field):
    total_len = coef_field.shape[-1]
    band_len = total_len >> LEVELS
    approx = coef_field[..., :band_len]
    for level_idx in range(LEVELS):
        detail = coef_field[..., band_len:2 * band_len]
        paired = jnp.stack(((approx + detail) * half_root, (approx - detail) * half_root), axis=-1)
        approx = paired.reshape(coef_field.shape[:-1] + (2 * band_len,))
        band_len = 2 * band_len
    return approx

def to_cells(coef_arr):
    along_first = synthesis(coef_arr)
    return synthesis(jnp.transpose(along_first, (2, 1, 0)))

def reference(observed, sens_tiles, tile_row, tile_owner, tile_block, coeffs, split_var, scaled_dual, lower_bound, upper_bound):
    coef_low = coeffs.astype(jnp.bfloat16)
    blocks_all = coef_low.reshape(N_ROW, CZC, N_SUB, CY, NX // TC, TC)
    blocks_all = jnp.transpose(blocks_all, (0, 2, 1, 3, 4, 5)).reshape(N_ROW, N_SUB, BLK_DEV, TC)
    sub_ids = jnp.arange(N_SUB, dtype=jnp.int32)[None, :, None]
    picked = blocks_all[tile_owner, sub_ids, tile_block]
    data_obs = observed.reshape(N_ROW, ROWB, TR)

    def forward_shard(inputs):
        tile_mats, coef_rows, row_ids = inputs
        products = jnp.einsum('stk,stki->sti', coef_rows.astype(jnp.float32), tile_mats.astype(jnp.float32))
        empty = jnp.zeros((ROWB, TR), jnp.float32)
        return empty.at[row_ids.reshape(-1)].add(products.reshape(-1, TR))
    predicted = lax.map(forward_shard, (sens_tiles, picked, tile_row))
    residual = predicted - data_obs
    misfit = 0.5 * jnp.mean(residual * residual)
    resid_low = residual.astype(jnp.bfloat16)

    def adjoint_shard(inputs):
        tile_mats, resid_rows, row_ids = inputs
        rows_used = resid_rows[row_ids]
        return jnp.einsum('stki,sti->stk', tile_mats.astype(jnp.float32), rows_used.astype(jnp.float32))
    contrib = lax.map(adjoint_shard, (sens_tiles, resid_low, tile_row))
    grad_blocks = jnp.zeros((N_ROW, N_SUB, BLK_DEV, TC), jnp.float32).at[tile_owner, sub_ids, tile_block].add(contrib)
    grad_blocks = grad_blocks.reshape(N_ROW, N_SUB, CZC, CY, NX // TC, TC)
    coef_grad = jnp.transpose(grad_blocks, (0, 2, 1, 3, 4, 5)).reshape(NZ, NY, NX)
    model_now = to_cells(coeffs)
    descent = to_cells(coef_grad)
    padded = jnp.pad(model_now, 1)
    beside = padded[2:, 1:-1, 1:-1] + padded[:-2, 1:-1, 1:-1]
    beside = beside + padded[1:-1, 2:, 1:-1] + padded[1:-1, :-2, 1:-1]
    beside = beside + padded[1:-1, 1:-1, 2:] + padded[1:-1, 1:-1, :-2]
    smooth = 6.0 * model_now - beside
    model_next = model_now - step_size * (data_weight * descent + smooth_weight * smooth + penalty * (model_now - split_var + scaled_dual))
    split_next = jnp.clip(model_next + scaled_dual, lower_bound, upper_bound)
    dual_next = scaled_dual + model_next - split_next
    primal_gap = model_next - split_next
    dual_gap = split_next - split_var
    primal = jnp.sqrt(jnp.mean(primal_gap * primal_gap))
    dual_norm = penalty * jnp.sqrt(jnp.mean(dual_gap * dual_gap))
    residual_norms = jnp.stack([misfit, primal, dual_norm])
    return (model_next, split_next, dual_next, residual_norms)
```

```python
import functools

import jax
import jax.numpy as jnp
import numpy as np
from jax import lax
from jax.experimental import pallas as pl
from jax.experimental.pallas import tpu as pltpu
from jax.sharding import PartitionSpec as P

LEVELS = 3
STEP = 0.1
SMOOTH_W = 0.5
DATA_W = 20.0
LANES = 128
MESH = pl.DeviceIdType.MESH
F32, BF16, I32 = jnp.float32, jnp.bfloat16, jnp.int32


def haar_pattern(n):
    pattern = np.zeros((n, n), np.float32)
    scale = np.zeros((n,), np.float64)
    cells = np.arange(n)
    base = n >> LEVELS
    for c in range(base):
        pattern[c, cells // 8 == c] = 1.0
        scale[c] = 2.0**-1.5
    for level in range(LEVELS, 0, -1):
        width = 1 << level
        start = n >> level
        for c in range(start):
            inside = cells // width == c
            sign = np.where((cells // (width // 2)) % 2 == 0, 1.0, -1.0)
            pattern[start + c] = np.where(inside, sign, 0.0)
            scale[start + c] = 2.0 ** (-0.5 * level)
    return pattern, scale.astype(np.float32)


def split_hi_lo(value):
    hi = value.astype(BF16)
    lo = (value - hi.astype(F32)).astype(BF16)
    return hi, lo


def dot_nt(a, b):
    return lax.dot_general(a, b, (((1,), (1,)), ((), ())), preferred_element_type=F32)


def dot_nn(a, b):
    return jnp.dot(a, b, preferred_element_type=F32)


def log2(n):
    return n.bit_length() - 1


def kernel(
    dims,
    row_ref,
    owner_ref,
    block_ref,
    obs_ref,
    coef_ref,
    px_ref,
    sx_ref,
    pz_ref,
    pzd_ref,
    szd_ref,
    sens_hbm,
    split_hbm,
    dual_hbm,
    lower_hbm,
    upper_hbm,
    next_ref,
    splitn_ref,
    dualn_ref,
    norm_ref,
    s3,
    split_v,
    dual_v,
    lower_v,
    upper_v,
    ids_all,
    vsend,
    pick_all,
    xs,
    mx_all,
    pred_all,
    contrib2,
    vt,
    v_all,
    model,
    ysend,
    xhalo,
    yhalo,
    zsel,
    norm_row,
    norm_sub,
    local_sem,
    row_send,
    row_recv,
    sub_send,
    sub_recv,
    halo_send,
    halo_recv,
):
    R, S, T, K, NX, NZ, CY, CZ, XL, RB, BLK = dims
    NXB = NX // K
    HALF = T // 2
    HY = LANES // CZ
    Q = CY // HY
    CELLS = XL * CY
    me_r = lax.axis_index("row")
    me_s = lax.axis_index("sub")

    def row_peer(d):
        return {"row": lax.rem(me_r + d, R)}

    def sub_peer(d):
        return {"sub": lax.rem(me_s + d, S)}

    loads = []
    for h in range(2):
        loads.append(
            pltpu.make_async_copy(
                sens_hbm.at[pl.ds(h * HALF, HALF)], s3.at[:, pl.ds(h * K, K), :], local_sem.at[h]
            )
        )
    cell_loads = []
    for n, (src, dst) in enumerate(
        ((split_hbm, split_v), (dual_hbm, dual_v), (lower_hbm, lower_v), (upper_hbm, upper_v))
    ):
        cell_loads.append(pltpu.make_async_copy(src, dst, local_sem.at[2 + n]))

    barrier = pltpu.get_barrier_semaphore()
    for d in range(1, R):
        pl.semaphore_signal(barrier, inc=1, device_id=row_peer(d), device_id_type=MESH)
    for d in range(1, S):
        pl.semaphore_signal(barrier, inc=1, device_id=sub_peer(d), device_id_type=MESH)
    for c in loads + cell_loads:
        c.start()

    gid = owner_ref[...] * BLK + block_ref[...]
    ids_all[me_r] = jnp.broadcast_to(gid, (8, T))
    pl.semaphore_wait(barrier, R - 1 + S - 1)

    def push_row(phase, src_of, dst):
        copies = []
        for d in range(1, R):
            c = pltpu.make_async_remote_copy(
                src_ref=src_of(lax.rem(me_r + d, R)),
                dst_ref=dst.at[me_r],
                send_sem=row_send.at[phase, d - 1],
                recv_sem=row_recv.at[phase, d - 1],
                device_id=row_peer(d),
                device_id_type=MESH,
            )
            c.start()
            copies.append(c)
        return copies

    def push_sub(phase, buf):
        copies = []
        for d in range(1, S):
            c = pltpu.make_async_remote_copy(
                src_ref=buf.at[me_s],
                dst_ref=buf.at[me_s],
                send_sem=sub_send.at[phase, d - 1],
                recv_sem=sub_recv.at[phase, d - 1],
                device_id=sub_peer(d),
                device_id_type=MESH,
            )
            c.start()
            copies.append(c)
        return copies

    sent = push_row(0, lambda r: ids_all.at[me_r], ids_all)

    sx = sx_ref[...]
    for q in range(Q):
        if NX > LANES:
            by_depth = coef_ref[...].reshape(CZ, CY, NX)
            parts = [by_depth[:, h * Q + q, :] for h in range(HY)]
        else:
            parts = [coef_ref[pl.ds(h * Q + q, CZ, stride=CY), :] for h in range(HY)]
        hi, lo = split_hi_lo(jnp.concatenate(parts, axis=0) * sx)
        xs[pl.ds(q, NX, stride=Q), :] = dot_nt(px_ref[...], hi) + dot_nt(px_ref[...], lo)
    low = coef_ref[...].astype(BF16)
    low_twice = []
    for xb in range(NXB):
        part = low[:, xb * K : (xb + 1) * K]
        low_twice.append(jnp.concatenate([part, part], axis=1))
    ZY = BLK // NXB
    lane = lax.broadcasted_iota(I32, (T, LANES), 1)
    first_half = lax.broadcasted_iota(I32, (HALF, LANES), 1) < K
    zy_lane = lax.broadcasted_iota(I32, (T, ZY), 1)
    zc_lane = lax.broadcasted_iota(I32, (T, NZ), 1)
    rows_col = jnp.transpose(jnp.broadcast_to(row_ref[...], (T, T)))
    rows2 = jnp.where(first_half, rows_col[:HALF], rows_col[HALF:])

    own_col = jnp.transpose(jnp.broadcast_to(gid, (T, T)))
    zc_own = lax.shift_right_logical(own_col, log2(CY * NXB))
    z_scale = jnp.where(
        zc_own < NZ // 4,
        2.0**-1.5,
        jnp.where(zc_own < NZ // 2, 0.5, 0.7071067811865476),
    ).astype(F32)
    tile_row_iota = lax.broadcasted_iota(I32, (T, LANES), 0)
    keep = (tile_row_iota < HALF) == (lane < K)
    z_scale = jnp.where(keep, z_scale * (STEP * DATA_W), 0.0)

    for c in sent:
        c.wait()
    cols = []
    for r in range(R):
        col = jnp.transpose(jnp.broadcast_to(ids_all[r, 0:1, :], (T, T)))
        cols.append(col)
        local = col - me_r * BLK
        wide = jnp.concatenate([local] * (ZY // T), axis=1)
        total = None
        for xb in range(NXB):
            hot = jnp.where(wide == zy_lane * NXB + xb, 1.0, 0.0).astype(BF16)
            value = dot_nn(hot, low_twice[xb])
            total = value if total is None else total + value
        vsend[r] = jnp.where(first_half, total[:HALF], total[HALF:]).astype(BF16)
    sent = push_row(1, lambda r: vsend.at[r], pick_all)
    pick_all[me_r] = vsend[me_r]
    bulk = push_row(2, lambda r: xs.at[pl.ds(pl.multiple_of(r * (XL * Q), XL * Q), XL * Q)], mx_all)
    mx_all[me_r] = xs[pl.ds(pl.multiple_of(me_r * (XL * Q), XL * Q), XL * Q), :]

    for r in range(R):
        zc = lax.shift_right_logical(cols[r], log2(CY * NXB))
        zc = jnp.concatenate([zc] * (NZ // T), axis=1)
        hot = jnp.where(zc == zc_lane, 1.0, 0.0).astype(BF16)
        zsel[pl.ds(r * T, T), :] = dot_nn(hot, pz_ref[...]).astype(BF16)

    for c in sent + loads:
        c.wait()
    picked = pick_all[0].astype(F32)
    for r in range(1, R):
        picked = picked + pick_all[r].astype(F32)
    b_iota = lax.broadcasted_iota(I32, (RB, LANES), 0)
    GROUP = 8
    pred = jnp.zeros((RB, T), F32)
    for g in range(HALF // GROUP):
        pieces = []
        for j in range(g * GROUP, (g + 1) * GROUP):
            hit = jnp.broadcast_to(rows2[j : j + 1, :], (RB, LANES)) == b_iota
            pieces.append(jnp.where(hit, jnp.broadcast_to(picked[j : j + 1, :], (RB, LANES)), 0.0))
        left = jnp.concatenate(pieces, axis=1).astype(BF16)
        right = s3[pl.ds(g * GROUP, GROUP)].reshape(GROUP * 2 * K, T)
        pred = pred + dot_nn(left, right)
    pred_all[me_s] = pred
    sent = push_sub(0, pred_all)

    for c in bulk:
        c.wait()
    r_iota = lax.broadcasted_iota(I32, (CELLS, LANES), 0)
    l_iota = lax.broadcasted_iota(I32, (CELLS, LANES), 1)
    own_lane = lax.shift_right_logical(l_iota, log2(CZ)) == lax.shift_right_logical(
        jnp.bitwise_and(r_iota, CY - 1), log2(Q)
    )
    lefts_hi, lefts_lo = [], []
    for r in range(R):
        m = mx_all[r] * szd_ref[r : r + 1, :]
        if Q == 1:
            m = jnp.broadcast_to(m.reshape(XL, 1, LANES), (XL, HY, LANES)).reshape(CELLS, LANES)
        else:
            m = jnp.broadcast_to(m.reshape(XL, 1, Q, LANES), (XL, HY, Q, LANES))
            m = m.reshape(CELLS, LANES)
        hi, lo = split_hi_lo(jnp.where(own_lane, m, 0.0))
        lefts_hi.append(hi)
        lefts_lo.append(lo)
    right = pzd_ref[...]
    now = dot_nn(jnp.concatenate(lefts_hi, axis=1), right) + dot_nn(
        jnp.concatenate(lefts_lo, axis=1), right
    )
    model[pl.ds(8, CELLS), :] = now
    ysend[0] = now.reshape(XL, CY, NZ)[:, 0, :]
    ysend[1] = now.reshape(XL, CY, NZ)[:, CY - 1, :]
    halos = []
    for n, (src, dst, peer) in enumerate(
        (
            (model.at[pl.ds(8, CY)], xhalo.at[1], row_peer(R - 1)),
            (model.at[pl.ds(8 + CELLS - CY, CY)], xhalo.at[0], row_peer(1)),
            (ysend.at[0], yhalo.at[1], sub_peer(S - 1)),
            (ysend.at[1], yhalo.at[0], sub_peer(1)),
        )
    ):
        c = pltpu.make_async_remote_copy(
            src_ref=src,
            dst_ref=dst,
            send_sem=halo_send.at[n],
            recv_sem=halo_recv.at[n],
            device_id=peer,
            device_id_type=MESH,
        )
        c.start()
        halos.append(c)

    for c in sent:
        c.wait()
    predicted = pred_all[0]
    for s in range(1, S):
        predicted = predicted + pred_all[s]
    residual = predicted - obs_ref[...]
    resid_low = residual.astype(BF16)
    for g in range(HALF // GROUP):
        right = s3[pl.ds(g * GROUP, GROUP)].reshape(GROUP * 2 * K, T)
        wide = dot_nt(resid_low, right)
        for n in range(GROUP):
            j = g * GROUP + n
            hit = jnp.broadcast_to(rows2[j : j + 1, :], (RB, LANES)) == b_iota
            piece = jnp.where(hit, wide[:, n * LANES : (n + 1) * LANES], 0.0)
            contrib2[j : j + 1, :] = jnp.sum(piece, axis=0, keepdims=True)
    c2 = contrib2[...]
    scaled = jnp.concatenate([c2, c2], axis=0) * z_scale
    vt_value = None
    for xb in range(NXB):
        part_sx = sx[:, xb * K : (xb + 1) * K]
        part_px = px_ref[:, xb * K : (xb + 1) * K]
        term = scaled * jnp.concatenate([part_sx, part_sx], axis=1)
        if NXB > 1:
            term = jnp.where(jnp.bitwise_and(own_col, NXB - 1) == xb, term, 0.0)
        hi, lo = split_hi_lo(term)
        twice = jnp.concatenate([part_px, part_px], axis=1)
        value = dot_nt(twice, hi) + dot_nt(twice, lo)
        vt_value = value if vt_value is None else vt_value + value
    vt[...] = vt_value
    sent = push_row(3, lambda r: vt.at[pl.ds(pl.multiple_of(r * XL, XL), XL)], v_all)
    v_all[me_r] = vt[pl.ds(pl.multiple_of(me_r * XL, XL), XL), :]

    for c in halos + cell_loads:
        c.wait()
    now = model[pl.ds(8, CELLS), :]
    x_lo = jnp.where(me_r > 0, xhalo[0], 0.0)
    x_hi = jnp.where(me_r < R - 1, xhalo[1], 0.0)
    beside = jnp.concatenate([x_lo, now[: CELLS - CY]], axis=0) + jnp.concatenate(
        [now[CY:], x_hi], axis=0
    )
    y_iota = jnp.bitwise_and(lax.broadcasted_iota(I32, (CELLS, NZ), 0), CY - 1)
    z_iota = lax.broadcasted_iota(I32, (CELLS, NZ), 1)

    def spread(edge):
        return jnp.broadcast_to(edge.reshape(XL, 1, NZ), (XL, CY, NZ)).reshape(CELLS, NZ)

    y_lo = spread(jnp.where(me_s > 0, yhalo[0], 0.0))
    y_hi = spread(jnp.where(me_s < S - 1, yhalo[1], 0.0))
    beside = beside + jnp.where(y_iota == 0, y_lo, pltpu.roll(now, 1, 0))
    beside = beside + jnp.where(y_iota == CY - 1, y_hi, pltpu.roll(now, CELLS - 1, 0))
    beside = beside + jnp.where(z_iota == 0, 0.0, pltpu.roll(now, 1, 1))
    beside = beside + jnp.where(z_iota == NZ - 1, 0.0, pltpu.roll(now, NZ - 1, 1))
    smooth = 6.0 * now - beside
    split_var = split_v[...]
    dual = dual_v[...]
    model[pl.ds(8, CELLS), :] = now - STEP * (SMOOTH_W * smooth + (now - split_var + dual))
    misfit_lane = jnp.sum(residual * residual, axis=0, keepdims=True)

    y_rows = lax.broadcasted_iota(I32, (CY, T), 0)
    y_hits = []
    for r in range(R):
        y_of = jnp.bitwise_and(lax.shift_right_logical(ids_all[r, 0:1, :], log2(NXB)), CY - 1)
        y_hits.append(jnp.where(jnp.broadcast_to(y_of, (CY, T)) == y_rows, 1.0, 0.0))

    for c in sent:
        c.wait()
    his, los = [], []
    for r in range(R):
        w = v_all[r].reshape(XL, 1, T) * y_hits[r].reshape(1, CY, T)
        hi, lo = split_hi_lo(w.reshape(CELLS, T))
        his.append(hi)
        los.append(lo)
    right = zsel[...]
    descent = dot_nn(jnp.concatenate(his, axis=1), right) + dot_nn(
        jnp.concatenate(los, axis=1), right
    )
    model_next = model[pl.ds(8, CELLS), :] - descent
    split_next = jnp.minimum(jnp.maximum(model_next + dual, lower_v[...]), upper_v[...])
    next_ref[...] = model_next
    splitn_ref[...] = split_next
    dualn_ref[...] = dual + model_next - split_next
    gap = model_next - split_next
    move = split_next - split_var
    gap = jnp.sum(gap * gap, axis=0, keepdims=True)
    move = jnp.sum(move * move, axis=0, keepdims=True)
    gap = sum(gap[:, n * LANES : (n + 1) * LANES] for n in range(NZ // LANES))
    move = sum(move[:, n * LANES : (n + 1) * LANES] for n in range(NZ // LANES))
    norm_row[me_r] = jnp.concatenate(
        [misfit_lane, gap, move, jnp.zeros((5, LANES), F32)], axis=0
    )
    for c in push_row(4, lambda r: norm_row.at[me_r], norm_row):
        c.wait()
    total = norm_row[0]
    for r in range(1, R):
        total = total + norm_row[r]
    norm_sub[me_s] = total
    for c in push_sub(1, norm_sub):
        c.wait()
    total = norm_sub[0]
    for s in range(1, S):
        total = total + norm_sub[s]
    total = jnp.broadcast_to(jnp.sum(total, axis=1, keepdims=True), (8, LANES))
    which = lax.broadcasted_iota(I32, (8, LANES), 0)
    cells = CELLS * NZ * R * S
    norm_ref[...] = jnp.where(
        which == 0, total * (0.5 / (RB * T * R * S)), jnp.sqrt(total * (1.0 / cells))
    )


def body(
    observed,
    sens_tiles,
    tile_row,
    tile_owner,
    tile_block,
    coeffs,
    split_var,
    scaled_dual,
    lower_bound,
    upper_bound,
):
    R = lax.axis_size("row")
    S = lax.axis_size("sub")
    T, K = sens_tiles.shape[2], sens_tiles.shape[3]
    CZ, CY, NX = coeffs.shape
    XL, _, NZ = split_var.shape
    RB = observed.shape[0]
    BLK = coeffs.size // K
    HY = LANES // CZ
    Q = CY // HY
    CELLS = XL * CY
    px, sx = haar_pattern(NX)
    pz, sz = haar_pattern(NZ)
    pzd = np.concatenate([np.tile(pz[r * CZ : (r + 1) * CZ], (HY, 1)) for r in range(R)], axis=0)
    szd = np.stack([np.tile(sz[r * CZ : (r + 1) * CZ], HY) for r in range(R)])
    dims = (R, S, T, K, NX, NZ, CY, CZ, XL, RB, BLK)
    vmem = pl.BlockSpec(memory_space=pltpu.VMEM)
    hbm = pl.BlockSpec(memory_space=pl.ANY)
    cell = jax.ShapeDtypeStruct((CELLS, NZ), F32)
    dma = pltpu.SemaphoreType.DMA
    outs = pl.pallas_call(
        functools.partial(kernel, dims),
        out_shape=[cell, cell, cell, jax.ShapeDtypeStruct((8, LANES), F32)],
        in_specs=[vmem] * 10 + [hbm] * 5,
        out_specs=[vmem] * 4,
        scratch_shapes=[
            pltpu.VMEM((T // 2, 2 * K, T), BF16),
            pltpu.VMEM((CELLS, NZ), F32),
            pltpu.VMEM((CELLS, NZ), F32),
            pltpu.VMEM((CELLS, NZ), F32),
            pltpu.VMEM((CELLS, NZ), F32),
            pltpu.VMEM((R, 8, T), I32),
            pltpu.VMEM((R, T // 2, LANES), BF16),
            pltpu.VMEM((R, T // 2, LANES), BF16),
            pltpu.VMEM((NX * Q, LANES), F32),
            pltpu.VMEM((R, XL * Q, LANES), F32),
            pltpu.VMEM((S, RB, T), F32),
            pltpu.VMEM((T // 2, LANES), F32),
            pltpu.VMEM((NX, T), F32),
            pltpu.VMEM((R, XL, T), F32),
            pltpu.VMEM((CELLS + 16, NZ), F32),
            pltpu.VMEM((2, XL, NZ), F32),
            pltpu.VMEM((2, CY, NZ), F32),
            pltpu.VMEM((2, XL, NZ), F32),
            pltpu.VMEM((R * T, NZ), BF16),
            pltpu.VMEM((R, 8, LANES), F32),
            pltpu.VMEM((S, 8, LANES), F32),
            dma((6,)),
            dma((5, R - 1)),
            dma((5, R - 1)),
            dma((2, S - 1)),
            dma((2, S - 1)),
            dma((4,)),
            dma((4,)),
        ],
        compiler_params=pltpu.CompilerParams(
            collective_id=0, has_side_effects=True, vmem_limit_bytes=48 * 1024 * 1024
        ),
        name="admm_step",
    )(
        tile_row.reshape(1, T),
        tile_owner.reshape(1, T),
        tile_block.reshape(1, T),
        observed,
        coeffs.reshape(CZ * CY, NX),
        jnp.asarray(px.T, BF16),
        jnp.asarray(sx[None, :], F32),
        jnp.asarray(pz, BF16),
        jnp.asarray(pzd, BF16),
        jnp.asarray(szd, F32),
        sens_tiles.reshape(T, K, T),
        split_var.reshape(CELLS, NZ),
        scaled_dual.reshape(CELLS, NZ),
        lower_bound.reshape(CELLS, NZ),
        upper_bound.reshape(CELLS, NZ),
    )
    model_next, split_next, dual_next = (o.reshape(split_var.shape) for o in outs[:3])
    return model_next, split_next, dual_next, outs[3][:3, 0]


def solution(mesh):
    in_specs = (
        P(("grp", "row"), None),
        P(("grp", "row"), "sub", None, None, None),
        P(("grp", "row"), "sub", None),
        P(("grp", "row"), "sub", None),
        P(("grp", "row"), "sub", None),
        P(("grp", "row"), "sub", None),
        P(("grp", "row"), "sub", None),
        P(("grp", "row"), "sub", None),
        P(("grp", "row"), "sub", None),
        P(("grp", "row"), "sub", None),
    )
    out_specs = (
        P(("grp", "row"), "sub", None),
        P(("grp", "row"), "sub", None),
        P(("grp", "row"), "sub", None),
        P("grp"),
    )
    return jax.shard_map(body, mesh=mesh, in_specs=in_specs, out_specs=out_specs, check_vma=False)
```

```python
import functools

import jax
import jax.numpy as jnp
import numpy as np
from jax import lax
from jax.experimental import pallas as pl
from jax.experimental.pallas import tpu as pltpu
from jax.sharding import PartitionSpec as P

LEVELS = 3
STEP = 0.1
SMOOTH_W = 0.5
DATA_W = 20.0
LANES = 128
MESH = pl.DeviceIdType.MESH
F32, BF16, I32 = jnp.float32, jnp.bfloat16, jnp.int32


def haar_pattern(n):
    pattern = np.zeros((n, n), np.float32)
    scale = np.zeros((n,), np.float64)
    cells = np.arange(n)
    base = n >> LEVELS
    for c in range(base):
        pattern[c, cells // 8 == c] = 1.0
        scale[c] = 2.0**-1.5
    for level in range(LEVELS, 0, -1):
        width = 1 << level
        start = n >> level
        for c in range(start):
            inside = cells // width == c
            sign = np.where((cells // (width // 2)) % 2 == 0, 1.0, -1.0)
            pattern[start + c] = np.where(inside, sign, 0.0)
            scale[start + c] = 2.0 ** (-0.5 * level)
    return pattern, scale.astype(np.float32)


def split_hi_lo(value):
    hi = value.astype(BF16)
    lo = (value - hi.astype(F32)).astype(BF16)
    return hi, lo


def dot_nt(a, b):
    return lax.dot_general(a, b, (((1,), (1,)), ((), ())), preferred_element_type=F32)


def dot_nn(a, b):
    return jnp.dot(a, b, preferred_element_type=F32)


def log2(n):
    return n.bit_length() - 1


def kernel(
    dims,
    row_hbm,
    owner_hbm,
    block_hbm,
    obs_hbm,
    coef_hbm,
    px_hbm,
    sx_hbm,
    pz_hbm,
    pzd_hbm,
    szd_hbm,
    sens_hbm,
    split_hbm,
    dual_hbm,
    lower_hbm,
    upper_hbm,
    shifted_ref,
    norm_ref,
    row_ref,
    owner_ref,
    block_ref,
    obs_ref,
    coef_ref,
    px_ref,
    sx_ref,
    pz_ref,
    pzd_ref,
    szd_ref,
    s3,
    split_v,
    dual_v,
    lower_v,
    upper_v,
    ids_all,
    vsend,
    pick_all,
    xs,
    mx_all,
    pred_all,
    contrib2,
    vt,
    v_all,
    model,
    ysend,
    xhalo,
    yhalo,
    zsel,
    norm_row,
    norm_sub,
    local_sem,
    row_send,
    row_recv,
    sub_send,
    sub_recv,
    halo_send,
    halo_recv,
):
    R, S, T, K, NX, NZ, CY, CZ, XL, RB, BLK = dims
    NXB = NX // K
    HALF = T // 2
    HY = LANES // CZ
    Q = CY // HY
    CELLS = XL * CY
    me_r = lax.axis_index("row")
    me_s = lax.axis_index("sub")

    def row_peer(d):
        return {"row": lax.rem(me_r + d, R)}

    def sub_peer(d):
        return {"sub": lax.rem(me_s + d, S)}

    first_loads = []
    for n, (src, dst) in enumerate(
        (
            (owner_hbm, owner_ref),
            (block_hbm, block_ref),
            (row_hbm, row_ref),
            (coef_hbm, coef_ref),
            (px_hbm, px_ref),
            (sx_hbm, sx_ref),
            (pz_hbm, pz_ref),
            (pzd_hbm, pzd_ref),
            (szd_hbm, szd_ref),
            (obs_hbm, obs_ref),
        )
    ):
        first_loads.append(pltpu.make_async_copy(src, dst, local_sem.at[6 + n]))
        first_loads[-1].start()

    loads = []
    for h in range(2):
        loads.append(
            pltpu.make_async_copy(
                sens_hbm.at[pl.ds(h * HALF, HALF)], s3.at[:, pl.ds(h * K, K), :], local_sem.at[h]
            )
        )
    cell_loads = []
    for n, (src, dst) in enumerate(
        ((split_hbm, split_v), (dual_hbm, dual_v), (lower_hbm, lower_v), (upper_hbm, upper_v))
    ):
        cell_loads.append(pltpu.make_async_copy(src, dst, local_sem.at[2 + n]))

    barrier = pltpu.get_barrier_semaphore()
    for d in range(1, R):
        pl.semaphore_signal(barrier, inc=1, device_id=row_peer(d), device_id_type=MESH)
    for d in range(1, S):
        pl.semaphore_signal(barrier, inc=1, device_id=sub_peer(d), device_id_type=MESH)
    for c in loads + cell_loads:
        c.start()

    for c in first_loads[:2]:
        c.wait()
    gid = owner_ref[...] * BLK + block_ref[...]
    ids_all[me_r] = jnp.broadcast_to(gid, (8, T))
    pl.semaphore_wait(barrier, R - 1 + S - 1)

    def push_row(phase, src_of, dst):
        copies = []
        for d in range(1, R):
            c = pltpu.make_async_remote_copy(
                src_ref=src_of(lax.rem(me_r + d, R)),
                dst_ref=dst.at[me_r],
                send_sem=row_send.at[phase, d - 1],
                recv_sem=row_recv.at[phase, d - 1],
                device_id=row_peer(d),
                device_id_type=MESH,
            )
            c.start()
            copies.append(c)
        return copies

    def push_sub(phase, buf):
        copies = []
        for d in range(1, S):
            c = pltpu.make_async_remote_copy(
                src_ref=buf.at[me_s],
                dst_ref=buf.at[me_s],
                send_sem=sub_send.at[phase, d - 1],
                recv_sem=sub_recv.at[phase, d - 1],
                device_id=sub_peer(d),
                device_id_type=MESH,
            )
            c.start()
            copies.append(c)
        return copies

    sent = push_row(0, lambda r: ids_all.at[me_r], ids_all)

    for c in first_loads[2:]:
        c.wait()
    sx = sx_ref[...]
    for q in range(Q):
        if NX > LANES:
            by_depth = coef_ref[...].reshape(CZ, CY, NX)
            parts = [by_depth[:, h * Q + q, :] for h in range(HY)]
        else:
            parts = [coef_ref[pl.ds(h * Q + q, CZ, stride=CY), :] for h in range(HY)]
        hi, lo = split_hi_lo(jnp.concatenate(parts, axis=0) * sx)
        xs[pl.ds(q, NX, stride=Q), :] = dot_nt(px_ref[...], hi) + dot_nt(px_ref[...], lo)
    low = coef_ref[...].astype(BF16)
    low_twice = []
    for xb in range(NXB):
        part = low[:, xb * K : (xb + 1) * K]
        low_twice.append(jnp.concatenate([part, part], axis=1))
    ZY = BLK // NXB
    lane = lax.broadcasted_iota(I32, (T, LANES), 1)
    first_half = lax.broadcasted_iota(I32, (HALF, LANES), 1) < K
    zy_lane = lax.broadcasted_iota(I32, (T, ZY), 1)
    zc_lane = lax.broadcasted_iota(I32, (T, NZ), 1)
    rows_col = jnp.transpose(jnp.broadcast_to(row_ref[...], (T, T)))
    rows2 = jnp.where(first_half, rows_col[:HALF], rows_col[HALF:])

    own_col = jnp.transpose(jnp.broadcast_to(gid, (T, T)))
    zc_own = lax.shift_right_logical(own_col, log2(CY * NXB))
    z_scale = jnp.where(
        zc_own < NZ // 4,
        2.0**-1.5,
        jnp.where(zc_own < NZ // 2, 0.5, 0.7071067811865476),
    ).astype(F32)
    tile_row_iota = lax.broadcasted_iota(I32, (T, LANES), 0)
    keep = (tile_row_iota < HALF) == (lane < K)
    z_scale = jnp.where(keep, z_scale * (STEP * DATA_W), 0.0)

    for c in sent:
        c.wait()
    cols = []
    for r in range(R):
        col = jnp.transpose(jnp.broadcast_to(ids_all[r, 0:1, :], (T, T)))
        cols.append(col)
        local = col - me_r * BLK
        wide = jnp.concatenate([local] * (ZY // T), axis=1)
        total = None
        for xb in range(NXB):
            hot = jnp.where(wide == zy_lane * NXB + xb, 1.0, 0.0).astype(BF16)
            value = dot_nn(hot, low_twice[xb])
            total = value if total is None else total + value
        vsend[r] = jnp.where(first_half, total[:HALF], total[HALF:]).astype(BF16)
    sent = push_row(1, lambda r: vsend.at[r], pick_all)
    pick_all[me_r] = vsend[me_r]
    bulk = push_row(2, lambda r: xs.at[pl.ds(pl.multiple_of(r * (XL * Q), XL * Q), XL * Q)], mx_all)
    mx_all[me_r] = xs[pl.ds(pl.multiple_of(me_r * (XL * Q), XL * Q), XL * Q), :]

    for r in range(R):
        zc = lax.shift_right_logical(cols[r], log2(CY * NXB))
        zc = jnp.concatenate([zc] * (NZ // T), axis=1)
        hot = jnp.where(zc == zc_lane, 1.0, 0.0).astype(BF16)
        zsel[pl.ds(r * T, T), :] = dot_nn(hot, pz_ref[...]).astype(BF16)

    for c in sent + loads:
        c.wait()
    picked = pick_all[0].astype(F32)
    for r in range(1, R):
        picked = picked + pick_all[r].astype(F32)
    b_iota = lax.broadcasted_iota(I32, (RB, LANES), 0)
    GROUP = 8
    pred = jnp.zeros((RB, T), F32)
    for g in range(HALF // GROUP):
        pieces = []
        for j in range(g * GROUP, (g + 1) * GROUP):
            hit = jnp.broadcast_to(rows2[j : j + 1, :], (RB, LANES)) == b_iota
            pieces.append(jnp.where(hit, jnp.broadcast_to(picked[j : j + 1, :], (RB, LANES)), 0.0))
        left = jnp.concatenate(pieces, axis=1).astype(BF16)
        right = s3[pl.ds(g * GROUP, GROUP)].reshape(GROUP * 2 * K, T)
        pred = pred + dot_nn(left, right)
    pred_all[me_s] = pred
    sent = push_sub(0, pred_all)

    for c in bulk:
        c.wait()
    r_iota = lax.broadcasted_iota(I32, (CELLS, LANES), 0)
    l_iota = lax.broadcasted_iota(I32, (CELLS, LANES), 1)
    own_lane = lax.shift_right_logical(l_iota, log2(CZ)) == lax.shift_right_logical(
        jnp.bitwise_and(r_iota, CY - 1), log2(Q)
    )
    lefts_hi, lefts_lo = [], []
    for r in range(R):
        m = mx_all[r] * szd_ref[r : r + 1, :]
        if Q == 1:
            m = jnp.broadcast_to(m.reshape(XL, 1, LANES), (XL, HY, LANES)).reshape(CELLS, LANES)
        else:
            m = jnp.broadcast_to(m.reshape(XL, 1, Q, LANES), (XL, HY, Q, LANES))
            m = m.reshape(CELLS, LANES)
        hi, lo = split_hi_lo(jnp.where(own_lane, m, 0.0))
        lefts_hi.append(hi)
        lefts_lo.append(lo)
    right = pzd_ref[...]
    now = dot_nn(jnp.concatenate(lefts_hi, axis=1), right) + dot_nn(
        jnp.concatenate(lefts_lo, axis=1), right
    )
    model[pl.ds(8, CELLS), :] = now
    ysend[0] = now.reshape(XL, CY, NZ)[:, 0, :]
    ysend[1] = now.reshape(XL, CY, NZ)[:, CY - 1, :]
    halos = []
    for n, (src, dst, peer) in enumerate(
        (
            (model.at[pl.ds(8, CY)], xhalo.at[1], row_peer(R - 1)),
            (model.at[pl.ds(8 + CELLS - CY, CY)], xhalo.at[0], row_peer(1)),
            (ysend.at[0], yhalo.at[1], sub_peer(S - 1)),
            (ysend.at[1], yhalo.at[0], sub_peer(1)),
        )
    ):
        c = pltpu.make_async_remote_copy(
            src_ref=src,
            dst_ref=dst,
            send_sem=halo_send.at[n],
            recv_sem=halo_recv.at[n],
            device_id=peer,
            device_id_type=MESH,
        )
        c.start()
        halos.append(c)

    for c in sent:
        c.wait()
    predicted = pred_all[0]
    for s in range(1, S):
        predicted = predicted + pred_all[s]
    residual = predicted - obs_ref[...]
    resid_low = residual.astype(BF16)
    for g in range(HALF // GROUP):
        right = s3[pl.ds(g * GROUP, GROUP)].reshape(GROUP * 2 * K, T)
        wide = dot_nt(resid_low, right)
        for n in range(GROUP):
            j = g * GROUP + n
            hit = jnp.broadcast_to(rows2[j : j + 1, :], (RB, LANES)) == b_iota
            piece = jnp.where(hit, wide[:, n * LANES : (n + 1) * LANES], 0.0)
            contrib2[j : j + 1, :] = jnp.sum(piece, axis=0, keepdims=True)
    c2 = contrib2[...]
    scaled = jnp.concatenate([c2, c2], axis=0) * z_scale
    vt_value = None
    for xb in range(NXB):
        part_sx = sx[:, xb * K : (xb + 1) * K]
        part_px = px_ref[:, xb * K : (xb + 1) * K]
        term = scaled * jnp.concatenate([part_sx, part_sx], axis=1)
        if NXB > 1:
            term = jnp.where(jnp.bitwise_and(own_col, NXB - 1) == xb, term, 0.0)
        hi, lo = split_hi_lo(term)
        twice = jnp.concatenate([part_px, part_px], axis=1)
        value = dot_nt(twice, hi) + dot_nt(twice, lo)
        vt_value = value if vt_value is None else vt_value + value
    vt[...] = vt_value
    sent = push_row(3, lambda r: vt.at[pl.ds(pl.multiple_of(r * XL, XL), XL)], v_all)
    v_all[me_r] = vt[pl.ds(pl.multiple_of(me_r * XL, XL), XL), :]

    for c in halos + cell_loads:
        c.wait()
    now = model[pl.ds(8, CELLS), :]
    x_lo = jnp.where(me_r > 0, xhalo[0], 0.0)
    x_hi = jnp.where(me_r < R - 1, xhalo[1], 0.0)
    beside = jnp.concatenate([x_lo, now[: CELLS - CY]], axis=0) + jnp.concatenate(
        [now[CY:], x_hi], axis=0
    )
    y_iota = jnp.bitwise_and(lax.broadcasted_iota(I32, (CELLS, NZ), 0), CY - 1)
    z_iota = lax.broadcasted_iota(I32, (CELLS, NZ), 1)

    def spread(edge):
        return jnp.broadcast_to(edge.reshape(XL, 1, NZ), (XL, CY, NZ)).reshape(CELLS, NZ)

    y_lo = spread(jnp.where(me_s > 0, yhalo[0], 0.0))
    y_hi = spread(jnp.where(me_s < S - 1, yhalo[1], 0.0))
    beside = beside + jnp.where(y_iota == 0, y_lo, pltpu.roll(now, 1, 0))
    beside = beside + jnp.where(y_iota == CY - 1, y_hi, pltpu.roll(now, CELLS - 1, 0))
    beside = beside + jnp.where(z_iota == 0, 0.0, pltpu.roll(now, 1, 1))
    beside = beside + jnp.where(z_iota == NZ - 1, 0.0, pltpu.roll(now, NZ - 1, 1))
    smooth = 6.0 * now - beside
    split_var = split_v[...]
    dual = dual_v[...]
    model[pl.ds(8, CELLS), :] = now - STEP * (SMOOTH_W * smooth + (now - split_var + dual))
    misfit_lane = jnp.sum(residual * residual, axis=0, keepdims=True)

    y_rows = lax.broadcasted_iota(I32, (CY, T), 0)
    y_hits = []
    for r in range(R):
        y_of = jnp.bitwise_and(lax.shift_right_logical(ids_all[r, 0:1, :], log2(NXB)), CY - 1)
        y_hits.append(jnp.where(jnp.broadcast_to(y_of, (CY, T)) == y_rows, 1.0, 0.0))

    for c in sent:
        c.wait()
    his, los = [], []
    for r in range(R):
        w = v_all[r].reshape(XL, 1, T) * y_hits[r].reshape(1, CY, T)
        hi, lo = split_hi_lo(w.reshape(CELLS, T))
        his.append(hi)
        los.append(lo)
    right = zsel[...]
    descent = dot_nn(jnp.concatenate(his, axis=1), right) + dot_nn(
        jnp.concatenate(los, axis=1), right
    )
    model_next = model[pl.ds(8, CELLS), :] - descent
    shifted = model_next + dual
    split_next = jnp.minimum(jnp.maximum(shifted, lower_v[...]), upper_v[...])
    gap = model_next - split_next
    move = split_next - split_var
    gap = jnp.sum(gap * gap, axis=0, keepdims=True)
    move = jnp.sum(move * move, axis=0, keepdims=True)
    gap = sum(gap[:, n * LANES : (n + 1) * LANES] for n in range(NZ // LANES))
    move = sum(move[:, n * LANES : (n + 1) * LANES] for n in range(NZ // LANES))
    norm_row[me_r] = jnp.concatenate(
        [misfit_lane, gap, move, jnp.zeros((5, LANES), F32)], axis=0
    )
    sent = push_row(4, lambda r: norm_row.at[me_r], norm_row)
    shifted_ref[...] = shifted
    for c in sent:
        c.wait()
    total = norm_row[0]
    for r in range(1, R):
        total = total + norm_row[r]
    norm_sub[me_s] = total
    for c in push_sub(1, norm_sub):
        c.wait()
    total = norm_sub[0]
    for s in range(1, S):
        total = total + norm_sub[s]
    total = jnp.broadcast_to(jnp.sum(total, axis=1, keepdims=True), (8, LANES))
    which = lax.broadcasted_iota(I32, (8, LANES), 0)
    cells = CELLS * NZ * R * S
    norm_ref[...] = jnp.where(
        which == 0, total * (0.5 / (RB * T * R * S)), jnp.sqrt(total * (1.0 / cells))
    )


def body(
    observed,
    sens_tiles,
    tile_row,
    tile_owner,
    tile_block,
    coeffs,
    split_var,
    scaled_dual,
    lower_bound,
    upper_bound,
):
    R = lax.axis_size("row")
    S = lax.axis_size("sub")
    T, K = sens_tiles.shape[2], sens_tiles.shape[3]
    CZ, CY, NX = coeffs.shape
    XL, _, NZ = split_var.shape
    RB = observed.shape[0]
    BLK = coeffs.size // K
    HY = LANES // CZ
    Q = CY // HY
    CELLS = XL * CY
    px, sx = haar_pattern(NX)
    pz, sz = haar_pattern(NZ)
    pzd = np.concatenate([np.tile(pz[r * CZ : (r + 1) * CZ], (HY, 1)) for r in range(R)], axis=0)
    szd = np.stack([np.tile(sz[r * CZ : (r + 1) * CZ], HY) for r in range(R)])
    dims = (R, S, T, K, NX, NZ, CY, CZ, XL, RB, BLK)
    vmem = pl.BlockSpec(memory_space=pltpu.VMEM)
    hbm = pl.BlockSpec(memory_space=pltpu.HBM)
    cell = jax.ShapeDtypeStruct((CELLS, NZ), F32)
    dma = pltpu.SemaphoreType.DMA
    outs = pl.pallas_call(
        functools.partial(kernel, dims),
        out_shape=[cell, jax.ShapeDtypeStruct((8, LANES), F32)],
        in_specs=[hbm] * 15,
        out_specs=[vmem] * 2,
        scratch_shapes=[
            pltpu.VMEM((1, T), I32),
            pltpu.VMEM((1, T), I32),
            pltpu.VMEM((1, T), I32),
            pltpu.VMEM((RB, T), F32),
            pltpu.VMEM((CZ * CY, NX), F32),
            pltpu.VMEM((NX, NX), BF16),
            pltpu.VMEM((1, NX), F32),
            pltpu.VMEM((NZ, NZ), BF16),
            pltpu.VMEM((R * LANES, NZ), BF16),
            pltpu.VMEM((R, LANES), F32),
            pltpu.VMEM((T // 2, 2 * K, T), BF16),
            pltpu.VMEM((CELLS, NZ), F32),
            pltpu.VMEM((CELLS, NZ), F32),
            pltpu.VMEM((CELLS, NZ), F32),
            pltpu.VMEM((CELLS, NZ), F32),
            pltpu.VMEM((R, 8, T), I32),
            pltpu.VMEM((R, T // 2, LANES), BF16),
            pltpu.VMEM((R, T // 2, LANES), BF16),
            pltpu.VMEM((NX * Q, LANES), F32),
            pltpu.VMEM((R, XL * Q, LANES), F32),
            pltpu.VMEM((S, RB, T), F32),
            pltpu.VMEM((T // 2, LANES), F32),
            pltpu.VMEM((NX, T), F32),
            pltpu.VMEM((R, XL, T), F32),
            pltpu.VMEM((CELLS + 16, NZ), F32),
            pltpu.VMEM((2, XL, NZ), F32),
            pltpu.VMEM((2, CY, NZ), F32),
            pltpu.VMEM((2, XL, NZ), F32),
            pltpu.VMEM((R * T, NZ), BF16),
            pltpu.VMEM((R, 8, LANES), F32),
            pltpu.VMEM((S, 8, LANES), F32),
            dma((16,)),
            dma((5, R - 1)),
            dma((5, R - 1)),
            dma((2, S - 1)),
            dma((2, S - 1)),
            dma((4,)),
            dma((4,)),
        ],
        compiler_params=pltpu.CompilerParams(
            collective_id=0, has_side_effects=True, vmem_limit_bytes=62 * 1024 * 1024
        ),
        name="admm_step",
    )(
        tile_row.reshape(1, T),
        tile_owner.reshape(1, T),
        tile_block.reshape(1, T),
        observed,
        coeffs.reshape(CZ * CY, NX),
        jnp.asarray(px.T, BF16),
        jnp.asarray(sx[None, :], F32),
        jnp.asarray(pz, BF16),
        jnp.asarray(pzd, BF16),
        jnp.asarray(szd, F32),
        sens_tiles.reshape(T, K, T),
        split_var.reshape(CELLS, NZ),
        scaled_dual.reshape(CELLS, NZ),
        lower_bound.reshape(CELLS, NZ),
        upper_bound.reshape(CELLS, NZ),
    )
    shifted = outs[0].reshape(split_var.shape)
    model_next = shifted - scaled_dual
    split_next = jnp.minimum(jnp.maximum(shifted, lower_bound), upper_bound)
    dual_next = shifted - split_next
    return model_next, split_next, dual_next, outs[1][:3, 0]


def solution(mesh):
    in_specs = (
        P(("grp", "row"), None),
        P(("grp", "row"), "sub", None, None, None),
        P(("grp", "row"), "sub", None),
        P(("grp", "row"), "sub", None),
        P(("grp", "row"), "sub", None),
        P(("grp", "row"), "sub", None),
        P(("grp", "row"), "sub", None),
        P(("grp", "row"), "sub", None),
        P(("grp", "row"), "sub", None),
        P(("grp", "row"), "sub", None),
    )
    out_specs = (
        P(("grp", "row"), "sub", None),
        P(("grp", "row"), "sub", None),
        P(("grp", "row"), "sub", None),
        P("grp"),
    )
    return jax.shard_map(body, mesh=mesh, in_specs=in_specs, out_specs=out_specs, check_vma=False)
```

```python
import functools

import jax
import jax.numpy as jnp
import numpy as np
from jax import lax
from jax.experimental import pallas as pl
from jax.experimental.pallas import tpu as pltpu
from jax.sharding import PartitionSpec as P

LEVELS = 3
STEP = 0.1
SMOOTH_W = 0.5
DATA_W = 20.0
LANES = 128
MESH = pl.DeviceIdType.MESH
F32, BF16, I32 = jnp.float32, jnp.bfloat16, jnp.int32


def haar_pattern(n):
    pattern = np.zeros((n, n), np.float32)
    scale = np.zeros((n,), np.float64)
    cells = np.arange(n)
    base = n >> LEVELS
    for c in range(base):
        pattern[c, cells // 8 == c] = 1.0
        scale[c] = 2.0**-1.5
    for level in range(LEVELS, 0, -1):
        width = 1 << level
        start = n >> level
        for c in range(start):
            inside = cells // width == c
            sign = np.where((cells // (width // 2)) % 2 == 0, 1.0, -1.0)
            pattern[start + c] = np.where(inside, sign, 0.0)
            scale[start + c] = 2.0 ** (-0.5 * level)
    return pattern, scale.astype(np.float32)


def split_hi_lo(value):
    hi = value.astype(BF16)
    lo = (value - hi.astype(F32)).astype(BF16)
    return hi, lo


def dot_nt(a, b):
    return lax.dot_general(a, b, (((1,), (1,)), ((), ())), preferred_element_type=F32)


def dot_nn(a, b):
    return jnp.dot(a, b, preferred_element_type=F32)


def log2(n):
    return n.bit_length() - 1


def kernel(
    dims,
    row_hbm,
    owner_hbm,
    block_hbm,
    obs_hbm,
    coef_hbm,
    px_hbm,
    sx_hbm,
    pz_hbm,
    pzd_hbm,
    szd_hbm,
    sens_hbm,
    split_hbm,
    dual_hbm,
    lower_hbm,
    upper_hbm,
    shifted_ref,
    norm_ref,
    row_ref,
    owner_ref,
    block_ref,
    obs_ref,
    coef_ref,
    px_ref,
    sx_ref,
    pz_ref,
    pzd_ref,
    szd_ref,
    s3,
    split_v,
    dual_v,
    lower_v,
    upper_v,
    ids_all,
    vsend,
    pick_all,
    xs,
    mx_all,
    pred_all,
    contrib2,
    vt,
    v_all,
    model,
    ysend,
    xhalo,
    yhalo,
    zsel,
    norm_row,
    norm_sub,
    norm_all,
    local_sem,
    row_send,
    row_recv,
    sub_send,
    sub_recv,
    halo_send,
    halo_recv,
    norm_send,
    norm_recv,
):
    R, S, T, K, NX, NZ, CY, CZ, XL, RB, BLK = dims
    NXB = NX // K
    HALF = T // 2
    HY = LANES // CZ
    Q = CY // HY
    CELLS = XL * CY
    me_r = lax.axis_index("row")
    me_s = lax.axis_index("sub")

    def row_peer(d):
        return {"row": lax.rem(me_r + d, R)}

    def sub_peer(d):
        return {"sub": lax.rem(me_s + d, S)}

    first_loads = []
    for n, (src, dst) in enumerate(
        (
            (owner_hbm, owner_ref),
            (block_hbm, block_ref),
            (row_hbm, row_ref),
            (coef_hbm, coef_ref),
            (px_hbm, px_ref),
            (sx_hbm, sx_ref),
            (pz_hbm, pz_ref),
            (pzd_hbm, pzd_ref),
            (szd_hbm, szd_ref),
            (obs_hbm, obs_ref),
        )
    ):
        first_loads.append(pltpu.make_async_copy(src, dst, local_sem.at[6 + n]))
        first_loads[-1].start()

    loads = []
    for h in range(2):
        loads.append(
            pltpu.make_async_copy(
                sens_hbm.at[pl.ds(h * HALF, HALF)], s3.at[:, pl.ds(h * K, K), :], local_sem.at[h]
            )
        )
    cell_loads = []
    for n, (src, dst) in enumerate(
        ((split_hbm, split_v), (dual_hbm, dual_v), (lower_hbm, lower_v), (upper_hbm, upper_v))
    ):
        cell_loads.append(pltpu.make_async_copy(src, dst, local_sem.at[2 + n]))

    barrier = pltpu.get_barrier_semaphore()
    direct = R * S <= 16
    if direct:
        all_peers = [
            {**row_peer(d), **sub_peer(e)} for d in range(R) for e in range(S) if d + e > 0
        ]
    near = [row_peer(d) for d in range(1, R)] + [sub_peer(d) for d in range(1, S)]
    for peer in near:
        pl.semaphore_signal(barrier, inc=1, device_id=peer, device_id_type=MESH)
    for c in loads + cell_loads:
        c.start()

    for c in first_loads[:2]:
        c.wait()
    gid = owner_ref[...] * BLK + block_ref[...]
    ids_all[me_r] = gid
    pl.semaphore_wait(barrier, len(near))

    def push_row(phase, src_of, dst):
        copies = []
        for d in range(1, R):
            c = pltpu.make_async_remote_copy(
                src_ref=src_of(lax.rem(me_r + d, R)),
                dst_ref=dst.at[me_r],
                send_sem=row_send.at[phase, d - 1],
                recv_sem=row_recv.at[phase, d - 1],
                device_id=row_peer(d),
                device_id_type=MESH,
            )
            c.start()
            copies.append(c)
        return copies

    def push_sub(phase, buf):
        copies = []
        for d in range(1, S):
            c = pltpu.make_async_remote_copy(
                src_ref=buf.at[me_s],
                dst_ref=buf.at[me_s],
                send_sem=sub_send.at[phase, d - 1],
                recv_sem=sub_recv.at[phase, d - 1],
                device_id=sub_peer(d),
                device_id_type=MESH,
            )
            c.start()
            copies.append(c)
        return copies

    sent = push_row(0, lambda r: ids_all.at[me_r], ids_all)

    for c in first_loads[2:]:
        c.wait()
    sx = sx_ref[...]
    for q in range(Q):
        if NX > LANES:
            by_depth = coef_ref[...].reshape(CZ, CY, NX)
            parts = [by_depth[:, h * Q + q, :] for h in range(HY)]
        else:
            parts = [coef_ref[pl.ds(h * Q + q, CZ, stride=CY), :] for h in range(HY)]
        hi, lo = split_hi_lo(jnp.concatenate(parts, axis=0) * sx)
        xs[pl.ds(q, NX, stride=Q), :] = dot_nt(px_ref[...], hi) + dot_nt(px_ref[...], lo)
    bulk = push_row(2, lambda r: xs.at[pl.ds(pl.multiple_of(r * (XL * Q), XL * Q), XL * Q)], mx_all)
    mx_all[me_r] = xs[pl.ds(pl.multiple_of(me_r * (XL * Q), XL * Q), XL * Q), :]
    low = coef_ref[...].astype(BF16)
    low_twice = []
    for xb in range(NXB):
        part = low[:, xb * K : (xb + 1) * K]
        low_twice.append(jnp.concatenate([part, part], axis=1))
    ZY = BLK // NXB
    lane = lax.broadcasted_iota(I32, (T, LANES), 1)
    first_half = lax.broadcasted_iota(I32, (HALF, LANES), 1) < K
    zy_lane = lax.broadcasted_iota(I32, (T, ZY), 1)
    zc_lane = lax.broadcasted_iota(I32, (T, NZ), 1)
    rows_col = jnp.transpose(jnp.broadcast_to(row_ref[...], (T, T)))
    rows2 = jnp.where(first_half, rows_col[:HALF], rows_col[HALF:])

    own_col = jnp.transpose(jnp.broadcast_to(gid, (T, T)))
    zc_own = lax.shift_right_logical(own_col, log2(CY * NXB))
    z_scale = jnp.where(
        zc_own < NZ // 4,
        2.0**-1.5,
        jnp.where(zc_own < NZ // 2, 0.5, 0.7071067811865476),
    ).astype(F32)
    tile_row_iota = lax.broadcasted_iota(I32, (T, LANES), 0)
    keep = (tile_row_iota < HALF) == (lane < K)
    z_scale = jnp.where(keep, z_scale * (STEP * DATA_W), 0.0)

    for c in sent:
        c.wait()
    cols = []
    for r in range(R):
        col = jnp.transpose(jnp.broadcast_to(ids_all[r, 0:1, :], (T, T)))
        cols.append(col)
        local = col - me_r * BLK
        wide = jnp.concatenate([local] * (ZY // T), axis=1)
        total = None
        for xb in range(NXB):
            hot = jnp.where(wide == zy_lane * NXB + xb, 1.0, 0.0).astype(BF16)
            value = dot_nn(hot, low_twice[xb])
            total = value if total is None else total + value
        vsend[r] = jnp.where(first_half, total[:HALF], total[HALF:]).astype(BF16)
    sent = push_row(1, lambda r: vsend.at[r], pick_all)
    pick_all[me_r] = vsend[me_r]

    for c in bulk:
        c.wait()
    r_iota = lax.broadcasted_iota(I32, (CELLS, LANES), 0)
    l_iota = lax.broadcasted_iota(I32, (CELLS, LANES), 1)
    own_lane = lax.shift_right_logical(l_iota, log2(CZ)) == lax.shift_right_logical(
        jnp.bitwise_and(r_iota, CY - 1), log2(Q)
    )
    lefts_hi, lefts_lo = [], []
    for r in range(R):
        m = mx_all[r] * szd_ref[r : r + 1, :]
        if Q == 1:
            m = jnp.broadcast_to(m.reshape(XL, 1, LANES), (XL, HY, LANES)).reshape(CELLS, LANES)
        else:
            m = jnp.broadcast_to(m.reshape(XL, 1, Q, LANES), (XL, HY, Q, LANES))
            m = m.reshape(CELLS, LANES)
        hi, lo = split_hi_lo(jnp.where(own_lane, m, 0.0))
        lefts_hi.append(hi)
        lefts_lo.append(lo)
    right = pzd_ref[...]
    now = dot_nn(jnp.concatenate(lefts_hi, axis=1), right) + dot_nn(
        jnp.concatenate(lefts_lo, axis=1), right
    )
    model[pl.ds(8, CELLS), :] = now
    ysend[0] = now.reshape(XL, CY, NZ)[:, 0, :]
    ysend[1] = now.reshape(XL, CY, NZ)[:, CY - 1, :]
    halos = []
    for n, (src, dst, peer) in enumerate(
        (
            (model.at[pl.ds(8, CY)], xhalo.at[1], row_peer(R - 1)),
            (model.at[pl.ds(8 + CELLS - CY, CY)], xhalo.at[0], row_peer(1)),
            (ysend.at[0], yhalo.at[1], sub_peer(S - 1)),
            (ysend.at[1], yhalo.at[0], sub_peer(1)),
        )
    ):
        c = pltpu.make_async_remote_copy(
            src_ref=src,
            dst_ref=dst,
            send_sem=halo_send.at[n],
            recv_sem=halo_recv.at[n],
            device_id=peer,
            device_id_type=MESH,
        )
        c.start()
        halos.append(c)

    for c in sent + loads:
        c.wait()
    picked = pick_all[0].astype(F32)
    for r in range(1, R):
        picked = picked + pick_all[r].astype(F32)
    b_iota = lax.broadcasted_iota(I32, (RB, LANES), 0)
    GROUP = 8
    pred = jnp.zeros((RB, T), F32)
    for g in range(HALF // GROUP):
        pieces = []
        for j in range(g * GROUP, (g + 1) * GROUP):
            hit = jnp.broadcast_to(rows2[j : j + 1, :], (RB, LANES)) == b_iota
            pieces.append(jnp.where(hit, jnp.broadcast_to(picked[j : j + 1, :], (RB, LANES)), 0.0))
        left = jnp.concatenate(pieces, axis=1).astype(BF16)
        right = s3[pl.ds(g * GROUP, GROUP)].reshape(GROUP * 2 * K, T)
        pred = pred + dot_nn(left, right)
    pred_all[me_s] = pred
    sent = push_sub(0, pred_all)

    for r in range(R):
        zc = lax.shift_right_logical(cols[r], log2(CY * NXB))
        zc = jnp.concatenate([zc] * (NZ // T), axis=1)
        hot = jnp.where(zc == zc_lane, 1.0, 0.0).astype(BF16)
        zsel[pl.ds(r * T, T), :] = dot_nn(hot, pz_ref[...]).astype(BF16)

    y_rows = lax.broadcasted_iota(I32, (CY, T), 0)
    y_hits = []
    for r in range(R):
        y_of = jnp.bitwise_and(lax.shift_right_logical(ids_all[r, 0:1, :], log2(NXB)), CY - 1)
        y_hits.append(jnp.where(jnp.broadcast_to(y_of, (CY, T)) == y_rows, 1.0, 0.0))

    for c in sent:
        c.wait()
    predicted = pred_all[0]
    for s in range(1, S):
        predicted = predicted + pred_all[s]
    residual = predicted - obs_ref[...]
    resid_low = residual.astype(BF16)
    for g in range(HALF // GROUP):
        right = s3[pl.ds(g * GROUP, GROUP)].reshape(GROUP * 2 * K, T)
        wide = dot_nt(resid_low, right)
        for n in range(GROUP):
            j = g * GROUP + n
            hit = jnp.broadcast_to(rows2[j : j + 1, :], (RB, LANES)) == b_iota
            piece = jnp.where(hit, wide[:, n * LANES : (n + 1) * LANES], 0.0)
            contrib2[j : j + 1, :] = jnp.sum(piece, axis=0, keepdims=True)
    c2 = contrib2[...]
    scaled = jnp.concatenate([c2, c2], axis=0) * z_scale
    vt_value = None
    for xb in range(NXB):
        part_sx = sx[:, xb * K : (xb + 1) * K]
        part_px = px_ref[:, xb * K : (xb + 1) * K]
        term = scaled * jnp.concatenate([part_sx, part_sx], axis=1)
        if NXB > 1:
            term = jnp.where(jnp.bitwise_and(own_col, NXB - 1) == xb, term, 0.0)
        hi, lo = split_hi_lo(term)
        twice = jnp.concatenate([part_px, part_px], axis=1)
        value = dot_nt(twice, hi) + dot_nt(twice, lo)
        vt_value = value if vt_value is None else vt_value + value
    vt[...] = vt_value
    sent = push_row(3, lambda r: vt.at[pl.ds(pl.multiple_of(r * XL, XL), XL)], v_all)
    v_all[me_r] = vt[pl.ds(pl.multiple_of(me_r * XL, XL), XL), :]

    for c in halos + cell_loads:
        c.wait()
    now = model[pl.ds(8, CELLS), :]
    x_lo = jnp.where(me_r > 0, xhalo[0], 0.0)
    x_hi = jnp.where(me_r < R - 1, xhalo[1], 0.0)
    beside = jnp.concatenate([x_lo, now[: CELLS - CY]], axis=0) + jnp.concatenate(
        [now[CY:], x_hi], axis=0
    )
    y_iota = jnp.bitwise_and(lax.broadcasted_iota(I32, (CELLS, NZ), 0), CY - 1)
    z_iota = lax.broadcasted_iota(I32, (CELLS, NZ), 1)

    def spread(edge):
        return jnp.broadcast_to(edge.reshape(XL, 1, NZ), (XL, CY, NZ)).reshape(CELLS, NZ)

    y_lo = spread(jnp.where(me_s > 0, yhalo[0], 0.0))
    y_hi = spread(jnp.where(me_s < S - 1, yhalo[1], 0.0))
    beside = beside + jnp.where(y_iota == 0, y_lo, pltpu.roll(now, 1, 0))
    beside = beside + jnp.where(y_iota == CY - 1, y_hi, pltpu.roll(now, CELLS - 1, 0))
    beside = beside + jnp.where(z_iota == 0, 0.0, pltpu.roll(now, 1, 1))
    beside = beside + jnp.where(z_iota == NZ - 1, 0.0, pltpu.roll(now, NZ - 1, 1))
    smooth = 6.0 * now - beside
    split_var = split_v[...]
    dual = dual_v[...]
    model[pl.ds(8, CELLS), :] = now - STEP * (SMOOTH_W * smooth + (now - split_var + dual))

    misfit_lane = jnp.sum(residual * residual, axis=0, keepdims=True)

    for c in sent:
        c.wait()
    his, los = [], []
    for r in range(R):
        w = v_all[r].reshape(XL, 1, T) * y_hits[r].reshape(1, CY, T)
        hi, lo = split_hi_lo(w.reshape(CELLS, T))
        his.append(hi)
        los.append(lo)
    right = zsel[...]
    descent = dot_nn(jnp.concatenate(his, axis=1), right) + dot_nn(
        jnp.concatenate(los, axis=1), right
    )
    model_next = model[pl.ds(8, CELLS), :] - descent
    shifted = model_next + dual
    split_next = jnp.minimum(jnp.maximum(shifted, lower_v[...]), upper_v[...])
    gap = model_next - split_next
    move = split_next - split_var
    gap = jnp.sum(gap * gap, axis=0, keepdims=True)
    move = jnp.sum(move * move, axis=0, keepdims=True)
    one = lax.broadcasted_iota(I32, (1, LANES), 1)
    sums = jnp.where(
        one == 0,
        jnp.sum(misfit_lane, axis=1, keepdims=True),
        jnp.where(
            one == 1, jnp.sum(gap, axis=1, keepdims=True), jnp.sum(move, axis=1, keepdims=True)
        ),
    )
    if direct:
        norm_all[me_r * S + me_s] = sums
        sent = []
        for n, peer in enumerate(all_peers):
            c = pltpu.make_async_remote_copy(
                src_ref=norm_all.at[me_r * S + me_s],
                dst_ref=norm_all.at[me_r * S + me_s],
                send_sem=norm_send.at[n],
                recv_sem=norm_recv.at[n],
                device_id=peer,
                device_id_type=MESH,
            )
            c.start()
            sent.append(c)
        shifted_ref[...] = shifted
        for c in sent:
            c.wait()
        total = norm_all[0]
        for n in range(1, R * S):
            total = total + norm_all[n]
    else:
        norm_row[me_r] = sums
        sent = push_row(4, lambda r: norm_row.at[me_r], norm_row)
        shifted_ref[...] = shifted
        for c in sent:
            c.wait()
        total = norm_row[0]
        for r in range(1, R):
            total = total + norm_row[r]
        norm_sub[me_s] = total
        for c in push_sub(1, norm_sub):
            c.wait()
        total = norm_sub[0]
        for s in range(1, S):
            total = total + norm_sub[s]
    cells = CELLS * NZ * R * S
    norm_ref[...] = jnp.where(
        one == 0, total * (0.5 / (RB * T * R * S)), jnp.sqrt(total * (1.0 / cells))
    )


def finish(shifted_ref, dual_ref, lower_ref, upper_ref, norm_ref, next_ref, split_ref, out_ref, norms_ref):
    shifted = shifted_ref[...]
    split_next = jnp.minimum(jnp.maximum(shifted, lower_ref[...]), upper_ref[...])
    next_ref[...] = shifted - dual_ref[...]
    split_ref[...] = split_next
    out_ref[...] = shifted - split_next
    for n in range(3):
        norms_ref[n] = norm_ref[0, n]


def body(
    observed,
    sens_tiles,
    tile_row,
    tile_owner,
    tile_block,
    coeffs,
    split_var,
    scaled_dual,
    lower_bound,
    upper_bound,
):
    R = lax.axis_size("row")
    S = lax.axis_size("sub")
    T, K = sens_tiles.shape[2], sens_tiles.shape[3]
    CZ, CY, NX = coeffs.shape
    XL, _, NZ = split_var.shape
    RB = observed.shape[0]
    BLK = coeffs.size // K
    HY = LANES // CZ
    Q = CY // HY
    CELLS = XL * CY
    px, sx = haar_pattern(NX)
    pz, sz = haar_pattern(NZ)
    pzd = np.concatenate([np.tile(pz[r * CZ : (r + 1) * CZ], (HY, 1)) for r in range(R)], axis=0)
    szd = np.stack([np.tile(sz[r * CZ : (r + 1) * CZ], HY) for r in range(R)])
    dims = (R, S, T, K, NX, NZ, CY, CZ, XL, RB, BLK)
    vmem = pl.BlockSpec(memory_space=pltpu.VMEM)
    hbm = pl.BlockSpec(memory_space=pltpu.HBM)
    cell = jax.ShapeDtypeStruct((CELLS, NZ), F32)
    dma = pltpu.SemaphoreType.DMA
    outs = pl.pallas_call(
        functools.partial(kernel, dims),
        out_shape=[cell, jax.ShapeDtypeStruct((1, LANES), F32)],
        in_specs=[hbm] * 15,
        out_specs=[vmem] * 2,
        scratch_shapes=[
            pltpu.VMEM((1, T), I32),
            pltpu.VMEM((1, T), I32),
            pltpu.VMEM((1, T), I32),
            pltpu.VMEM((RB, T), F32),
            pltpu.VMEM((CZ * CY, NX), F32),
            pltpu.VMEM((NX, NX), BF16),
            pltpu.VMEM((1, NX), F32),
            pltpu.VMEM((NZ, NZ), BF16),
            pltpu.VMEM((R * LANES, NZ), BF16),
            pltpu.VMEM((R, LANES), F32),
            pltpu.VMEM((T // 2, 2 * K, T), BF16),
            pltpu.VMEM((CELLS, NZ), F32),
            pltpu.VMEM((CELLS, NZ), F32),
            pltpu.VMEM((CELLS, NZ), F32),
            pltpu.VMEM((CELLS, NZ), F32),
            pltpu.VMEM((R, 1, T), I32),
            pltpu.VMEM((R, T // 2, LANES), BF16),
            pltpu.VMEM((R, T // 2, LANES), BF16),
            pltpu.VMEM((NX * Q, LANES), F32),
            pltpu.VMEM((R, XL * Q, LANES), F32),
            pltpu.VMEM((S, RB, T), F32),
            pltpu.VMEM((T // 2, LANES), F32),
            pltpu.VMEM((NX, T), F32),
            pltpu.VMEM((R, XL, T), F32),
            pltpu.VMEM((CELLS + 16, NZ), F32),
            pltpu.VMEM((2, XL, NZ), F32),
            pltpu.VMEM((2, CY, NZ), F32),
            pltpu.VMEM((2, XL, NZ), F32),
            pltpu.VMEM((R * T, NZ), BF16),
            pltpu.VMEM((R, 1, LANES), F32),
            pltpu.VMEM((S, 1, LANES), F32),
            pltpu.VMEM((R * S, 1, LANES), F32),
            dma((16,)),
            dma((5, R - 1)),
            dma((5, R - 1)),
            dma((2, S - 1)),
            dma((2, S - 1)),
            dma((4,)),
            dma((4,)),
            dma((R * S - 1,)),
            dma((R * S - 1,)),
        ],
        compiler_params=pltpu.CompilerParams(
            collective_id=0, has_side_effects=True, vmem_limit_bytes=62 * 1024 * 1024
        ),
        name="admm_step",
    )(
        tile_row.reshape(1, T),
        tile_owner.reshape(1, T),
        tile_block.reshape(1, T),
        observed,
        coeffs.reshape(CZ * CY, NX),
        jnp.asarray(px.T, BF16),
        jnp.asarray(sx[None, :], F32),
        jnp.asarray(pz, BF16),
        jnp.asarray(pzd, BF16),
        jnp.asarray(szd, F32),
        sens_tiles.reshape(T, K, T),
        split_var.reshape(CELLS, NZ),
        scaled_dual.reshape(CELLS, NZ),
        lower_bound.reshape(CELLS, NZ),
        upper_bound.reshape(CELLS, NZ),
    )
    smem = pl.BlockSpec(memory_space=pltpu.SMEM)
    model_next, split_next, dual_next, norms = pl.pallas_call(
        finish,
        out_shape=[cell, cell, cell, jax.ShapeDtypeStruct((3,), F32)],
        in_specs=[vmem] * 4 + [smem],
        out_specs=[vmem] * 3 + [smem],
        name="cell_outputs",
    )(
        outs[0],
        scaled_dual.reshape(CELLS, NZ),
        lower_bound.reshape(CELLS, NZ),
        upper_bound.reshape(CELLS, NZ),
        outs[1],
    )
    shape = split_var.shape
    return model_next.reshape(shape), split_next.reshape(shape), dual_next.reshape(shape), norms


def solution(mesh):
    in_specs = (
        P(("grp", "row"), None),
        P(("grp", "row"), "sub", None, None, None),
        P(("grp", "row"), "sub", None),
        P(("grp", "row"), "sub", None),
        P(("grp", "row"), "sub", None),
        P(("grp", "row"), "sub", None),
        P(("grp", "row"), "sub", None),
        P(("grp", "row"), "sub", None),
        P(("grp", "row"), "sub", None),
        P(("grp", "row"), "sub", None),
    )
    out_specs = (
        P(("grp", "row"), "sub", None),
        P(("grp", "row"), "sub", None),
        P(("grp", "row"), "sub", None),
        P("grp"),
    )
    return jax.shard_map(body, mesh=mesh, in_specs=in_specs, out_specs=out_specs, check_vma=False)
```
